128 devices in a mesh: dp: 16 (over x_hi, z, core), tensor: 8 (over x_lo, y).
Axes of the slice: x: 4 (x_hi: 2, x_lo: 2; x = x_hi * 2 + x_lo), y: 4, z: 4, core: 2. Of those that a mesh axis runs over, the one named last changes fastest.
Arguments:
- policy_input: bfloat16 [16384, 8192], P('dp', 'tensor'), may hold values from -6 to 6
- frozen_input: bfloat16 [16384, 8192], P('dp', 'tensor'), may hold values from -6 to 6
- policy_query: bfloat16 [16384, 8192], P('dp', 'tensor'), may hold values from -360 to 360
- frozen_query: bfloat16 [16384, 8192], P('dp', 'tensor'), may hold values from -360 to 360
- readout: bfloat16 [16384, 8192], P('dp', 'tensor'), may hold values from -0.29882812 to 0.29882812
- policy_weight: bfloat16 [8192, 2048], P('tensor', 'dp'), may hold values from -0.0625 to 0.0625
- frozen_weight: bfloat16 [8192, 2048], P('tensor', 'dp'), may hold values from -0.0625 to 0.0625
- resp_start: int32 [16, 2], P('dp'), may hold values from 1 to 128
- valid_len: int32 [16, 2], P('dp'), may hold values from 256 to 512
Outputs:
- total_loss: float32 [], replicated
- grad_weight: float32 [8192, 2048], P('tensor', 'dp')
- grad_input: bfloat16 [16384, 8192], P('dp', 'tensor')
The draws below stay inside these ranges and needn't reach their ends.
All inputs are finite; a program needn't handle non-finite values.
Results may differ from the reference program's by a relative error of at most 0.018.
Values may be sent and summed in bfloat16 or wider, within the bound.
No kernel may reach another device: no remote copies, remote signals or barrier semaphores. Data moves between devices by JAX's collectives and lax.ppermute only.
A program may use at most 192 MiB of HBM per device.

```python
import math
import jax
import jax.numpy as jnp
from jax import lax

D = 8192
H = 64
KVH = 8
HD = 128
LEN = 512
PAIRS = 16
TOKENS = 16384


def spread_rows(key, widest):
    first, second = jax.random.split(key)
    base = jnp.clip(jax.random.normal(first, (TOKENS, H * HD), jnp.float32), -6.0, 6.0)
    levels = jnp.exp(jax.random.uniform(second, (TOKENS, 1), jnp.float32, 0.0, math.log(widest)))
    return (base * levels).astype(jnp.bfloat16)


def draw_policy_query(key, part):
    key = jax.random.fold_in(key, 11)
    return spread_rows(key, 1.0)


def draw_frozen_query(key, part):
    key = jax.random.fold_in(key, 23)
    return spread_rows(key, 1.0)


def place_ends(array, rng, least, high):
    shape = array.shape
    place = [jax.random.randint(jax.random.fold_in(rng, axis), (), 0, shape[axis]) for axis in range(len(shape))]
    array = array.at[tuple(place)].set(least)
    longest = shape.index(max(shape))
    place[longest] = (place[longest] + 1) % shape[longest]
    return array.at[tuple(place)].set(high)


def block_scale(key, extent, cuts, low, top_value):
    gain, own = 1.0, jax.random.fold_in(key, 6)
    for dim, shards_of in cuts:
        heights = jnp.exp(jax.random.uniform(jax.random.fold_in(own, dim), (shards_of,), jnp.float32, low / len(cuts), top_value / len(cuts)))
        gain = gain * jnp.repeat(heights, extent[dim] // shards_of).reshape([-1 if axis == dim else 1 for axis in range(len(extent))])
    return gain


def centred(own_key, dims, deviation, reach, cuts=(), kind=jnp.bfloat16):
    result = deviation * jax.random.normal(own_key, dims, jnp.float32)
    if cuts:
        result = result * block_scale(own_key, dims, cuts, -0.22, 0.18)
    return jnp.clip(result, -reach, reach).astype(kind)


def setup_inputs(seed: int = 0) -> dict:
    streams_of = jax.random.split(jax.random.key(seed), 10)
    policy_input = centred(streams_of[0], (TOKENS, D), 1.0, 6.0, ((0, 16), (1, 8)))
    frozen_input = centred(streams_of[1], (TOKENS, D), 1.0, 6.0, ((0, 16), (1, 8)))
    policy_query = draw_policy_query(jax.random.fold_in(streams_of[9], 71), 0)
    frozen_query = draw_frozen_query(jax.random.fold_in(streams_of[9], 71), 0)
    readout = centred(streams_of[4], (TOKENS, H * HD), 0.05, 0.29882812, ((0, 16), (1, 8)))
    policy_weight = centred(streams_of[5], (D, 2 * KVH * HD), D ** -0.5, 0.0625, ((0, 8), (1, 16)))
    frozen_weight = centred(streams_of[6], (D, 2 * KVH * HD), D ** -0.5, 0.0625, ((0, 8), (1, 16)))
    resp_start = place_ends(jax.random.randint(streams_of[7], (PAIRS, 2), 1, LEN // 4 + 1), jax.random.fold_in(streams_of[7], 1), 1, (LEN // 4 + 1) - 1).astype(jnp.int32)
    valid_len = place_ends(jax.random.randint(streams_of[8], (PAIRS, 2), LEN // 2, LEN + 1), jax.random.fold_in(streams_of[8], 1), LEN // 2, LEN).astype(jnp.int32)
    return dict(policy_input=policy_input, frozen_input=frozen_input, policy_query=policy_query, frozen_query=frozen_query, readout=readout, policy_weight=policy_weight, frozen_weight=frozen_weight, resp_start=resp_start, valid_len=valid_len)


BETA = 0.1
NEGATIVE = -1e+30
EXACT = lax.Precision.HIGHEST

def attend_seq(query, keyval, readout, valid, begin):
    length = query.shape[0]
    factor = query.shape[-1] ** (-0.5)
    keys = keyval[:, :, 0].astype(jnp.float32)
    values = keyval[:, :, 1].astype(jnp.float32)
    scores = jnp.einsum('ikrd,jkd->krij', query.astype(jnp.float32), keys, precision=EXACT) * factor
    places = jnp.arange(length)
    allowed = (places[None, :] <= places[:, None]) & (places[None, :] < valid)
    scores = jnp.where(allowed, scores, NEGATIVE)
    highest = lax.optimization_barrier(jnp.max(scores, axis=-1, keepdims=True))
    expons = jnp.exp(scores - highest)
    weights = expons / lax.optimization_barrier(jnp.sum(expons, axis=-1, keepdims=True))
    rounded = lax.optimization_barrier(weights.astype(jnp.bfloat16))
    mixed = jnp.einsum('krij,jkd->ikrd', rounded.astype(jnp.float32), values, precision=EXACT)
    token_lp = lax.optimization_barrier(jnp.sum(mixed * readout.astype(jnp.float32), axis=(1, 2, 3)))
    answer = (places >= begin) & (places < valid)
    return (weights, rounded, mixed, token_lp, answer)

def backward_seq(query, keyval, weights, rounded, mixed, readout, answer, seq_factor):
    factor = query.shape[-1] ** (-0.5)
    values = keyval[:, :, 1].astype(jnp.float32)
    scaled = jnp.where(answer, seq_factor, 0.0)
    upstream = lax.optimization_barrier((scaled[:, None, None, None] * readout.astype(jnp.float32)).astype(jnp.bfloat16))
    upwide = upstream.astype(jnp.float32)
    dvalues = jnp.einsum('krij,ikrd->jkd', rounded.astype(jnp.float32), upwide, precision=EXACT)
    dweights = jnp.einsum('ikrd,jkd->krij', upwide, values, precision=EXACT)
    inner = jnp.einsum('ikrd,ikrd->kri', upwide, mixed, precision=EXACT)
    dscores = lax.optimization_barrier((weights * (dweights - inner[..., None])).astype(jnp.bfloat16))
    dkeys = jnp.einsum('krij,ikrd->jkd', dscores.astype(jnp.float32), query.astype(jnp.float32), precision=EXACT) * factor
    return jnp.stack([dkeys, dvalues], axis=2).astype(jnp.bfloat16)

def reference(policy_input, frozen_input, policy_query, frozen_query, readout, policy_weight, frozen_weight, resp_start, valid_len):
    groups = H // KVH
    count = 2 * PAIRS

    def kv_heads(flat):
        return flat.reshape(count, LEN, KVH, 2, HD)

    def q_heads(flat):
        return flat.reshape(count, LEN, KVH, groups, HD)
    policy_kv = kv_heads(jnp.dot(policy_input, policy_weight, preferred_element_type=jnp.float32))
    frozen_kv = kv_heads(jnp.dot(frozen_input, frozen_weight, preferred_element_type=jnp.float32))
    policy_q = q_heads(policy_query)
    frozen_q = q_heads(frozen_query)
    reading = q_heads(readout)
    valid = valid_len.reshape(count)
    begin = resp_start.reshape(count)

    def seq_logprob(items):
        query, keyval, read, vlen, first = items
        _, _, _, token_lp, answer = attend_seq(query, keyval, read, vlen, first)
        return jnp.sum(jnp.where(answer, token_lp, 0.0))
    policy_lp = lax.map(seq_logprob, (policy_q, policy_kv, reading, valid, begin)).reshape(PAIRS, 2)
    frozen_lp = lax.map(seq_logprob, (frozen_q, frozen_kv, reading, valid, begin)).reshape(PAIRS, 2)
    margin = BETA * (policy_lp[:, 0] - frozen_lp[:, 0] - (policy_lp[:, 1] - frozen_lp[:, 1]))
    total_loss = jnp.sum(jax.nn.softplus(-margin))
    sigmas = jax.nn.sigmoid(-margin)
    factors = jnp.stack([-BETA * sigmas, BETA * sigmas], axis=1).reshape(count)

    def seq_grad(items):
        query, keyval, read, vlen, first, seq_factor = items
        weights, rounded, mixed, _, answer = attend_seq(query, keyval, read, vlen, first)
        return backward_seq(query, keyval, weights, rounded, mixed, read, answer, seq_factor)
    dkeyval = lax.map(seq_grad, (policy_q, policy_kv, reading, valid, begin, factors)).reshape(count * LEN, 2 * KVH * HD)
    grad_weight = lax.dot_general(policy_input, dkeyval, (((0,), (0,)), ((), ())), preferred_element_type=jnp.float32)
    grad_input = lax.dot_general(dkeyval, policy_weight, (((1,), (1,)), ((), ())), preferred_element_type=jnp.float32).astype(jnp.bfloat16)
    return (total_loss, grad_weight, grad_input)
```

```python
import functools
import jax
import jax.numpy as jnp
from jax import lax
from jax.experimental import pallas as pl
from jax.experimental.pallas import tpu as pltpu
from jax.sharding import PartitionSpec as P

HD = 128
LEN = 512
HALF = LEN // 2
GROUPS = 8
LOG2E = 1.4426950408889634
NEGATIVE = -1e30
BETA = 0.1


def split_pair(wide):
    high = wide.astype(jnp.bfloat16)
    low = (wide - high.astype(jnp.float32)).astype(jnp.bfloat16)
    return jnp.concatenate([high, low], axis=1)


def nt(a, b):
    return lax.dot_general(a, b, (((1,), (1,)), ((), ())), preferred_element_type=jnp.float32)


def nn(a, b):
    return jnp.dot(a, b, preferred_element_type=jnp.float32)


def softmax_over_rows(scores, unit):
    highest = jnp.max(scores, axis=0, keepdims=True)
    expons = jnp.exp2((scores - highest) * unit)
    return expons * (1.0 / jnp.sum(expons, axis=0, keepdims=True))


def masked_scores(keys, query, block, valid):
    scores = nt(keys, jnp.concatenate([query, query], axis=1))
    rows = lax.broadcasted_iota(jnp.int32, (HALF, HALF), 0)
    cols = lax.broadcasted_iota(jnp.int32, (HALF, HALF), 1)
    if block == 0:
        return jnp.where(rows <= cols, scores, NEGATIVE)
    tail = jnp.where((rows <= cols) & (rows < valid - HALF), scores[HALF:], NEGATIVE)
    return jnp.concatenate([scores[:HALF], tail], axis=0)


def answered(block, begin, valid, read):
    places = lax.broadcasted_iota(jnp.int32, (HALF, 1), 0) + block * HALF
    return jnp.where((places >= begin) & (places < valid), read, jnp.zeros_like(read))


def policy_kernel(per, ends, kv_ref, q_ref, r_ref, dkv_ref, lp_ref, keys, values, dk, dv):
    seq, head = pl.program_id(0), pl.program_id(1)
    begin, valid = ends[0, seq], ends[1, seq]
    factor = HD ** (-0.5)

    @pl.when(head == 0)
    def _():
        keys[...] = split_pair(kv_ref[:, :HD])
        values[...] = split_pair(kv_ref[:, HD:])
        dk[...] = jnp.zeros_like(dk)
        dv[...] = jnp.zeros_like(dv)
        lp_ref[...] = jnp.zeros_like(lp_ref)

    lp = jnp.zeros((1, HALF), jnp.float32)
    for h in range(per):
        for block in range(2):
            span = (block + 1) * HALF
            rows = slice(block * HALF, span)
            query = q_ref[rows, h * HD : (h + 1) * HD]
            read = answered(block, begin, valid, r_ref[rows, h * HD : (h + 1) * HD])
            weights = softmax_over_rows(
                masked_scores(keys[:span], query, block, valid), factor * LOG2E
            )
            rounded = weights.astype(jnp.bfloat16)
            dweights = nt(values[:span], jnp.concatenate([read, read], axis=1))
            inner = jnp.sum(rounded.astype(jnp.float32) * dweights, axis=0, keepdims=True)
            lp = lp + inner
            dscores = (weights * (dweights - inner)).astype(jnp.bfloat16)
            dv[:span] += nn(rounded, read)
            dk[:span] += nn(dscores, query)
    lp_ref[0, :1, :] += lp

    @pl.when(head == pl.num_programs(1) - 1)
    def _():
        dkv_ref[:, :HD] = (dk[...] * factor).astype(jnp.bfloat16)
        dkv_ref[:, HD:] = dv[...].astype(jnp.bfloat16)


def frozen_kernel(per, ends, kv_ref, q_ref, r_ref, lp_ref, keys, values):
    seq, head = pl.program_id(0), pl.program_id(1)
    begin, valid = ends[0, seq], ends[1, seq]
    factor = HD ** (-0.5)

    @pl.when(head == 0)
    def _():
        keys[...] = split_pair(kv_ref[:, :HD])
        values[...] = split_pair(kv_ref[:, HD:])
        lp_ref[...] = jnp.zeros_like(lp_ref)

    lp = jnp.zeros((1, HALF), jnp.float32)
    for h in range(per):
        for block in range(2):
            span = (block + 1) * HALF
            rows = slice(block * HALF, span)
            query = q_ref[rows, h * HD : (h + 1) * HD]
            read = answered(block, begin, valid, r_ref[rows, h * HD : (h + 1) * HD])
            weights = softmax_over_rows(
                masked_scores(keys[:span], query, block, valid), factor * LOG2E
            )
            rounded = weights.astype(jnp.bfloat16)
            dweights = nt(values[:span], jnp.concatenate([read, read], axis=1))
            lp = lp + jnp.sum(rounded.astype(jnp.float32) * dweights, axis=0, keepdims=True)
    lp_ref[0, :1, :] += lp


def attention(policy, kv, query, readout, ends, per=4):
    steps = GROUPS // per
    rows = lambda s, h, *_: (s, 0)
    block = lambda s, h, *_: (s, h)
    kernel = policy_kernel if policy else frozen_kernel
    lp_shape = jax.ShapeDtypeStruct((2, 8, HALF), jnp.float32)
    lp_spec = pl.BlockSpec((1, 8, HALF), lambda s, h, *_: (s, 0, 0))
    scratch = [pltpu.VMEM((LEN, 2 * HD), jnp.bfloat16)] * 2
    flops = 2 * GROUPS * LEN * LEN * HD * 2 * (6 if policy else 4)
    if policy:
        out_shape = (jax.ShapeDtypeStruct((2 * LEN, 2 * HD), jnp.bfloat16), lp_shape)
        out_specs = (pl.BlockSpec((LEN, 2 * HD), rows), lp_spec)
        scratch = scratch + [pltpu.VMEM((LEN, HD), jnp.float32)] * 2
    else:
        out_shape, out_specs = lp_shape, lp_spec
    out = pl.pallas_call(
        functools.partial(kernel, per),
        out_shape=out_shape,
        grid_spec=pltpu.PrefetchScalarGridSpec(
            num_scalar_prefetch=1,
            grid=(2, steps),
            in_specs=[
                pl.BlockSpec((LEN, 2 * HD), rows),
                pl.BlockSpec((LEN, per * HD), block),
                pl.BlockSpec((LEN, per * HD), block),
            ],
            out_specs=out_specs,
            scratch_shapes=scratch,
        ),
        compiler_params=pltpu.CompilerParams(vmem_limit_bytes=32 * 2**20),
        cost_estimate=pl.CostEstimate(
            flops=flops, bytes_accessed=5 * 2**20, transcendentals=2 * GROUPS * LEN * LEN
        ),
        name="policy_attention" if policy else "frozen_attention",
    )(ends, kv, query, readout)
    return out


def tensor_perm(value, dx, dy):
    return lax.ppermute(
        value,
        "tensor",
        [(x * 4 + y, (x ^ dx) * 4 + (y - dy) % 4) for x in range(2) for y in range(4)],
    )


def dp_perm(value, dx, dz, dc=0):
    return lax.ppermute(
        value,
        "dp",
        [
            (x * 8 + z * 2 + c, (x ^ dx) * 8 + (z - dz) % 4 * 2 + (c ^ dc))
            for x in range(2)
            for z in range(4)
            for c in range(2)
        ],
    )


def sum_tensor(value):
    value = value + tensor_perm(value, 1, 0)
    ahead = [tensor_perm(value, 0, k) for k in (1, 2, 3)]
    return (value + ahead[1]) + (ahead[0] + ahead[2])


def sum_dp(value):
    value = value + dp_perm(value, 0, 0, 1)
    value = value + dp_perm(value, 1, 0)
    ahead = [dp_perm(value, 0, k) for k in (1, 2, 3)]
    return (value + ahead[1]) + (ahead[0] + ahead[2])


def triple(wide):
    keys = wide[:, :HD]
    high = keys.astype(jnp.bfloat16)
    low = (keys - high.astype(jnp.float32)).astype(jnp.bfloat16)
    return jnp.concatenate([high, low, wide[:, HD:].astype(jnp.bfloat16)], axis=1)


def untriple(sent):
    wide = sent.astype(jnp.float32)
    return jnp.concatenate([wide[:, :HD] + wide[:, HD : 2 * HD], wide[:, 2 * HD :]], axis=1)


def far_kernel(span, order, x_ref, k_ref, v_ref, *outs):
    step = pl.program_id(0)
    part = triple(nn(x_ref[span], jnp.concatenate([k_ref[0], v_ref[0]], axis=1)))
    for k, out in enumerate(outs):

        @pl.when(step == k)
        def _(out=out):
            out[...] = part


def side_kernel(span, order, x_ref, k_ref, v_ref, two, one, three, local):
    step = pl.program_id(0)
    part = nn(x_ref[span], jnp.concatenate([k_ref[0], v_ref[0]], axis=1))
    for k, out in enumerate((two, one, three)):

        @pl.when(step // 2 == k)
        def _(out=out):
            out[step % 2] = triple(part)

    @pl.when(step // 2 == 3)
    def _():
        local[step % 2] = part


def near_kernel(final, span, order, x_ref, k_ref, v_ref, got, out):
    part = nn(x_ref[span], jnp.concatenate([k_ref[0], v_ref[0]], axis=1)) + untriple(got[...])
    out[...] = part if final else triple(part)


def whole(shape):
    return pl.BlockSpec(shape, lambda *_: (0,) * len(shape))


def project(kernel, order, x, stack, rows, heads, outs, extra=()):
    tokens, features = x.shape
    picks = jnp.stack([order[h] for h in heads])
    weight = (1, features, HD)
    return pl.pallas_call(
        kernel,
        out_shape=outs,
        grid_spec=pltpu.PrefetchScalarGridSpec(
            num_scalar_prefetch=1,
            grid=(len(heads),),
            in_specs=[
                whole((tokens, features)),
                pl.BlockSpec(weight, lambda i, o: (o[i, 0], 0, 0)),
                pl.BlockSpec(weight, lambda i, o: (o[i, 1], 0, 0)),
            ]
            + [whole(e.shape) for e in extra],
            out_specs=jax.tree.map(lambda s: whole(s.shape), outs),
        ),
        compiler_params=pltpu.CompilerParams(vmem_limit_bytes=32 * 2**20),
        cost_estimate=pl.CostEstimate(
            flops=2 * rows * features * 2 * HD * len(heads),
            bytes_accessed=2 * rows * features + 8 * features * HD * len(heads),
            transcendentals=0,
        ),
    )(picks, x, stack, stack, *extra)


def side_sum_kernel(local, two, one, three, keep, send):
    keep[...] = local[0] + (untriple(two[0]) + untriple(one[0])) + untriple(three[0])
    send[...] = triple(local[1] + (untriple(two[1]) + untriple(one[1])) + untriple(three[1]))


def join_kernel(local, two, one, three, side, got, out):
    first = local.shape[0]
    out[:first] = local[...] + (untriple(two[...]) + untriple(one[...])) + untriple(three[...])
    out[first:] = side[...] + untriple(got[...])


def call_whole(kernel, outs, *args):
    moved = sum(a.size * a.dtype.itemsize for a in args)
    return pl.pallas_call(
        kernel,
        out_shape=outs,
        compiler_params=pltpu.CompilerParams(vmem_limit_bytes=32 * 2**20),
        cost_estimate=pl.CostEstimate(flops=moved, bytes_accessed=2 * moved, transcendentals=0),
    )(*args)


FIRST = 576


def reduce_heads(x, stack, order):
    tokens = x.shape[0]
    rest = tokens - FIRST
    near, side = slice(0, FIRST), slice(FIRST, tokens)
    shape = jax.ShapeDtypeStruct
    sent = shape((FIRST, 3 * HD), jnp.bfloat16)
    kept = shape((FIRST, 2 * HD), jnp.float32)
    two_sent = shape((2, rest, 3 * HD), jnp.bfloat16)
    two_kept = shape((2, rest, 2 * HD), jnp.float32)
    turn = (2, 1, 3, 0)
    far = project(
        functools.partial(far_kernel, near), order, x, stack, FIRST, [4 + k for k in turn], (sent,) * 4
    )
    got = [tensor_perm(f, 1, 0) for f in far]
    *sides, local = project(
        functools.partial(side_kernel, side),
        order,
        x,
        stack,
        rest,
        [d * 4 + k for k in turn for d in range(2)],
        (two_sent,) * 3 + (two_kept,),
    )
    back = [tensor_perm(s, 0, 4 - k) for s, k in zip(sides, turn)]
    mine = []
    for k, g in zip(turn, got):
        part = project(
            functools.partial(near_kernel, k == 0, near), order, x, stack, FIRST, [k], kept if k == 0 else sent, (g,)
        )
        mine.append(part if k == 0 else tensor_perm(part, 0, 4 - k))
    keep, send = call_whole(
        side_sum_kernel,
        (shape((rest, 2 * HD), jnp.float32), shape((rest, 3 * HD), jnp.bfloat16)),
        local,
        *back,
    )
    cross = tensor_perm(send, 1, 0)
    return call_whole(
        join_kernel, shape((tokens, 2 * HD), jnp.float32), mine[3], mine[0], mine[1], mine[2], keep, cross
    )


def weight_pieces(weight):
    across = dp_perm(weight, 1, 0)
    mine = [weight] + [dp_perm(weight, 0, k) for k in (1, 2, 3)]
    mine += [across] + [dp_perm(across, 0, k) for k in (1, 2, 3)]
    return jnp.stack(mine + [dp_perm(m, 0, 0, 1) for m in mine])


def grad_weight_kernel(picks, core, factors, xt_ref, d_ref, own_ref, other_ref):
    half = xt_ref.shape[1] // 2
    part = factors[0] * nn(xt_ref[:, :half], d_ref[0, :half])
    part = (part + factors[1] * nn(xt_ref[:, half:], d_ref[0, half:])).astype(jnp.bfloat16)
    keys, values = part[:, :HD], part[:, HD:]
    own_ref[0] = jnp.where(core[0] == 0, keys, values)
    other_ref[0] = jnp.where(core[0] == 0, values, keys)


def grad_weight_terms(xt, dkv, picks, core, factors):
    features, tokens = xt.shape
    out = jax.ShapeDtypeStruct((8, features, HD), jnp.bfloat16)
    spec = pl.BlockSpec((1, features, HD), lambda i, *_: (i, 0, 0))
    return pl.pallas_call(
        grad_weight_kernel,
        out_shape=(out, out),
        grid_spec=pltpu.PrefetchScalarGridSpec(
            num_scalar_prefetch=3,
            grid=(8,),
            in_specs=[
                whole(xt.shape),
                pl.BlockSpec((1, tokens, 2 * HD), lambda i, p, *_: (p[i], 0, 0)),
            ],
            out_specs=(spec, spec),
        ),
        compiler_params=pltpu.CompilerParams(vmem_limit_bytes=32 * 2**20),
        cost_estimate=pl.CostEstimate(
            flops=2 * features * tokens * 16 * HD, bytes_accessed=10 * 2**20, transcendentals=0
        ),
    )(picks, core, factors, xt, dkv)


def grad_input_kernel(order, factors, d_ref, w_ref, out_ref, turned):
    seq = pl.program_id(0)

    @pl.when(seq == 0)
    def _():
        for head in range(8):
            for kind in range(2):
                at = (2 * head + kind) * HD
                turned[:, at : at + HD] = w_ref[order[head, kind]]

    rows = jnp.concatenate([d_ref[head] for head in range(8)], axis=1)
    out_ref[...] = (factors[seq] * nt(rows, turned[...])).astype(jnp.bfloat16)


def grad_input_of(dkv, stack, order, factors):
    tokens, features = dkv.shape[1], stack.shape[1]
    half = tokens // 2
    return pl.pallas_call(
        grad_input_kernel,
        out_shape=jax.ShapeDtypeStruct((tokens, features), jnp.bfloat16),
        grid_spec=pltpu.PrefetchScalarGridSpec(
            num_scalar_prefetch=2,
            grid=(2,),
            in_specs=[pl.BlockSpec((8, half, 2 * HD), lambda s, *_: (0, s, 0)), whole(stack.shape)],
            out_specs=pl.BlockSpec((half, features), lambda s, *_: (s, 0)),
            scratch_shapes=[pltpu.VMEM((features, 16 * HD), jnp.bfloat16)],
        ),
        compiler_params=pltpu.CompilerParams(vmem_limit_bytes=40 * 2**20),
        cost_estimate=pl.CostEstimate(
            flops=2 * features * tokens * 16 * HD, bytes_accessed=12 * 2**20, transcendentals=0
        ),
    )(order, factors, dkv, stack)


def spread_heads(dkv):
    half = dkv.shape[0] // 2
    a, b = dkv[:half], dkv[half:]
    ya = [a] + [tensor_perm(a, 0, k) for k in (1, 2, 3)]
    xb = tensor_perm(b, 1, 0)
    xa = [tensor_perm(m, 1, 0) for m in ya]
    yb = [b] + [tensor_perm(b, 0, k) for k in (1, 2, 3)]
    yb += [xb] + [tensor_perm(xb, 0, k) for k in (1, 2, 3)]
    return jnp.stack([jnp.concatenate(pair) for pair in zip(ya + xa, yb)])


def reduce_terms(own, other):
    total = own + dp_perm(other, 0, 0, 1)
    got = [dp_perm(total[k], k // 4, (4 - k % 4) % 4) for k in range(1, 8)]
    out = total[0].astype(jnp.float32)
    for g in got:
        out = out + g.astype(jnp.float32)
    return out


def on_device(
    policy_input,
    frozen_input,
    policy_query,
    frozen_query,
    readout,
    policy_weight,
    frozen_weight,
    resp_start,
    valid_len,
):
    place, head = lax.axis_index("dp"), lax.axis_index("tensor")
    x_hi, z, core = place // 8, place // 2 % 4, place % 2
    x_lo, y = head // 4, head % 4
    ends = jnp.concatenate([resp_start, valid_len], axis=0)
    near = jnp.arange(8, dtype=jnp.int32)
    heads = (x_lo ^ (near // 4)) * 4 + (y + near) % 4
    places = ((heads // 4) ^ x_hi) * 4 + (heads - z) % 4
    order = jnp.stack([places + 8 * core, places + 8 * (1 - core)], axis=1).astype(jnp.int32)
    frozen_order = jnp.stack([2 * heads, 2 * heads + 1], axis=1).astype(jnp.int32)
    targets = (x_hi ^ (near // 4)) * 4 + (z + near) % 4
    picks = (((targets // 4) ^ x_lo) * 4 + (targets - y) % 4).astype(jnp.int32)

    policy_stack = weight_pieces(policy_weight)
    frozen_stack = lax.all_gather(frozen_weight, "dp")
    policy_kv = reduce_heads(policy_input, policy_stack, order)
    dkv, policy_sums = attention(True, policy_kv, policy_query, readout, ends)
    frozen_kv = reduce_heads(frozen_input, frozen_stack, frozen_order)
    frozen_sums = attention(False, frozen_kv, frozen_query, readout, ends)
    gap = jnp.sum(policy_sums - frozen_sums, axis=(1, 2))
    gap = sum_tensor(jnp.broadcast_to(gap[:, None], (2, HD)))[:, 0]
    margin = BETA * (gap[0] - gap[1])
    total_loss = sum_dp(jnp.broadcast_to(jax.nn.softplus(-margin), (1, HD)))[0, 0]
    sigma = jax.nn.sigmoid(-margin)
    factors = jnp.stack([-BETA * sigma, BETA * sigma])
    dkv_all = spread_heads(dkv)
    own, other = grad_weight_terms(
        policy_input.T, dkv_all, picks, core.astype(jnp.int32).reshape(1), factors
    )
    grad_weight = reduce_terms(own, other)
    grad_input = grad_input_of(dkv_all, policy_stack, order, factors)
    return (total_loss, grad_weight, grad_input)


def solution(mesh):
    in_specs = (
        P("dp", "tensor"),
        P("dp", "tensor"),
        P("dp", "tensor"),
        P("dp", "tensor"),
        P("dp", "tensor"),
        P("tensor", "dp"),
        P("tensor", "dp"),
        P("dp", None),
        P("dp", None),
    )
    out_specs = (P(), P("tensor", "dp"), P("dp", "tensor"))
    return jax.shard_map(
        on_device, mesh=mesh, in_specs=in_specs, out_specs=out_specs, check_vma=False
    )
```

```python
import functools
import jax
import jax.numpy as jnp
from jax import lax
from jax.experimental import pallas as pl
from jax.experimental.pallas import tpu as pltpu
from jax.sharding import PartitionSpec as P

HD = 128
LEN = 512
HALF = LEN // 2
GROUPS = 8
LOG2E = 1.4426950408889634
NEGATIVE = -1e30
BETA = 0.1


def split_pair(wide):
    high = wide.astype(jnp.bfloat16)
    low = (wide - high.astype(jnp.float32)).astype(jnp.bfloat16)
    return jnp.concatenate([high, low], axis=1)


def nt(a, b):
    return lax.dot_general(a, b, (((1,), (1,)), ((), ())), preferred_element_type=jnp.float32)


def nn(a, b):
    return jnp.dot(a, b, preferred_element_type=jnp.float32)


def softmax_over_rows(scores, unit):
    highest = jnp.max(scores, axis=0, keepdims=True)
    expons = jnp.exp2((scores - highest) * unit)
    return expons * (1.0 / jnp.sum(expons, axis=0, keepdims=True))


def masked_scores(keys, query, block, valid):
    scores = nt(keys, jnp.concatenate([query, query], axis=1))
    rows = lax.broadcasted_iota(jnp.int32, (HALF, HALF), 0)
    cols = lax.broadcasted_iota(jnp.int32, (HALF, HALF), 1)
    if block == 0:
        return jnp.where(rows <= cols, scores, NEGATIVE)
    tail = jnp.where((rows <= cols) & (rows < valid - HALF), scores[HALF:], NEGATIVE)
    return jnp.concatenate([scores[:HALF], tail], axis=0)


def answered(block, begin, valid, read):
    places = lax.broadcasted_iota(jnp.int32, (HALF, 1), 0) + block * HALF
    return jnp.where((places >= begin) & (places < valid), read, jnp.zeros_like(read))


def policy_kernel(per, seq, ends, kv_ref, q_ref, r_ref, dkv_ref, lp_ref, keys, values, dk, dv):
    head = pl.program_id(0)
    begin, valid = ends[0, seq], ends[1, seq]
    factor = HD ** (-0.5)

    @pl.when(head == 0)
    def _():
        keys[...] = split_pair(kv_ref[:, :HD])
        values[...] = split_pair(kv_ref[:, HD:])
        dk[...] = jnp.zeros_like(dk)
        dv[...] = jnp.zeros_like(dv)
        lp_ref[...] = jnp.zeros_like(lp_ref)

    lp = jnp.zeros((1, HALF), jnp.float32)
    for h in range(per):
        for block in range(2):
            span = (block + 1) * HALF
            rows = slice(block * HALF, span)
            query = q_ref[rows, h * HD : (h + 1) * HD]
            read = answered(block, begin, valid, r_ref[rows, h * HD : (h + 1) * HD])
            weights = softmax_over_rows(
                masked_scores(keys[:span], query, block, valid), factor * LOG2E
            )
            rounded = weights.astype(jnp.bfloat16)
            dweights = nt(values[:span], jnp.concatenate([read, read], axis=1))
            inner = jnp.sum(rounded.astype(jnp.float32) * dweights, axis=0, keepdims=True)
            lp = lp + inner
            dscores = (weights * (dweights - inner)).astype(jnp.bfloat16)
            dv[:span] += nn(rounded, read)
            dk[:span] += nn(dscores, query)
    lp_ref[:1, :] += lp

    @pl.when(head == pl.num_programs(0) - 1)
    def _():
        dkv_ref[:, :HD] = (dk[...] * factor).astype(jnp.bfloat16)
        dkv_ref[:, HD:] = dv[...].astype(jnp.bfloat16)


def frozen_kernel(per, seq, ends, kv_ref, q_ref, r_ref, lp_ref, keys, values):
    head = pl.program_id(0)
    begin, valid = ends[0, seq], ends[1, seq]
    factor = HD ** (-0.5)

    @pl.when(head == 0)
    def _():
        keys[...] = split_pair(kv_ref[:, :HD])
        values[...] = split_pair(kv_ref[:, HD:])
        lp_ref[...] = jnp.zeros_like(lp_ref)

    lp = jnp.zeros((1, HALF), jnp.float32)
    for h in range(per):
        for block in range(2):
            span = (block + 1) * HALF
            rows = slice(block * HALF, span)
            query = q_ref[rows, h * HD : (h + 1) * HD]
            read = answered(block, begin, valid, r_ref[rows, h * HD : (h + 1) * HD])
            weights = softmax_over_rows(
                masked_scores(keys[:span], query, block, valid), factor * LOG2E
            )
            rounded = weights.astype(jnp.bfloat16)
            dweights = nt(values[:span], jnp.concatenate([read, read], axis=1))
            lp = lp + jnp.sum(rounded.astype(jnp.float32) * dweights, axis=0, keepdims=True)
    lp_ref[:1, :] += lp


def attention(policy, seq, kv, query, readout, ends, per=4):
    steps = GROUPS // per
    rows = lambda h, *_: (seq, 0)
    block = lambda h, *_: (seq, h)
    kernel = policy_kernel if policy else frozen_kernel
    lp_shape = jax.ShapeDtypeStruct((8, HALF), jnp.float32)
    lp_spec = pl.BlockSpec((8, HALF), lambda h, *_: (0, 0))
    scratch = [pltpu.VMEM((LEN, 2 * HD), jnp.bfloat16)] * 2
    flops = GROUPS * LEN * LEN * HD * 2 * (6 if policy else 4)
    if policy:
        out_shape = (jax.ShapeDtypeStruct((LEN, 2 * HD), jnp.bfloat16), lp_shape)
        out_specs = (pl.BlockSpec((LEN, 2 * HD), lambda h, *_: (0, 0)), lp_spec)
        scratch = scratch + [pltpu.VMEM((LEN, HD), jnp.float32)] * 2
    else:
        out_shape, out_specs = lp_shape, lp_spec
    out = pl.pallas_call(
        functools.partial(kernel, per, seq),
        out_shape=out_shape,
        grid_spec=pltpu.PrefetchScalarGridSpec(
            num_scalar_prefetch=1,
            grid=(steps,),
            in_specs=[
                pl.BlockSpec((LEN, 2 * HD), rows),
                pl.BlockSpec((LEN, per * HD), block),
                pl.BlockSpec((LEN, per * HD), block),
            ],
            out_specs=out_specs,
            scratch_shapes=scratch,
        ),
        compiler_params=pltpu.CompilerParams(vmem_limit_bytes=32 * 2**20),
        cost_estimate=pl.CostEstimate(
            flops=flops, bytes_accessed=5 * 2**19, transcendentals=GROUPS * LEN * LEN
        ),
        name="policy_attention" if policy else "frozen_attention",
    )(ends, kv, query, readout)
    return out


def tensor_perm(value, dx, dy):
    return lax.ppermute(
        value,
        "tensor",
        [(x * 4 + y, (x ^ dx) * 4 + (y - dy) % 4) for x in range(2) for y in range(4)],
    )


def dp_perm(value, dx, dz, dc=0):
    return lax.ppermute(
        value,
        "dp",
        [
            (x * 8 + z * 2 + c, (x ^ dx) * 8 + (z - dz) % 4 * 2 + (c ^ dc))
            for x in range(2)
            for z in range(4)
            for c in range(2)
        ],
    )


def sum_tensor(value):
    value = value + tensor_perm(value, 1, 0)
    ahead = [tensor_perm(value, 0, k) for k in (1, 2, 3)]
    return (value + ahead[1]) + (ahead[0] + ahead[2])


def triple(wide):
    keys = wide[:, :HD]
    high = keys.astype(jnp.bfloat16)
    low = (keys - high.astype(jnp.float32)).astype(jnp.bfloat16)
    return jnp.concatenate([high, low, wide[:, HD:].astype(jnp.bfloat16)], axis=1)


def untriple(sent):
    wide = sent.astype(jnp.float32)
    return jnp.concatenate([wide[:, :HD] + wide[:, HD : 2 * HD], wide[:, 2 * HD :]], axis=1)


def far_kernel(span, order, x_ref, k_ref, v_ref, *outs):
    step = pl.program_id(0)
    part = triple(nn(x_ref[span], jnp.concatenate([k_ref[0], v_ref[0]], axis=1)))
    for k, out in enumerate(outs):

        @pl.when(step == k)
        def _(out=out):
            out[...] = part


def side_kernel(span, order, x_ref, k_ref, v_ref, two, one, three, local):
    step = pl.program_id(0)
    part = nn(x_ref[span], jnp.concatenate([k_ref[0], v_ref[0]], axis=1))
    for k, out in enumerate((two, one, three)):

        @pl.when(step // 2 == k)
        def _(out=out):
            out[step % 2] = triple(part)

    @pl.when(step // 2 == 3)
    def _():
        local[step % 2] = part


def near_kernel(final, span, order, x_ref, k_ref, v_ref, got, out):
    part = nn(x_ref[span], jnp.concatenate([k_ref[0], v_ref[0]], axis=1)) + untriple(got[...])
    out[...] = part if final else triple(part)


def whole(shape):
    return pl.BlockSpec(shape, lambda *_: (0,) * len(shape))


def project(kernel, order, x, stack, rows, heads, outs, extra=()):
    tokens, features = x.shape
    picks = jnp.stack([order[h] for h in heads])
    weight = (1, features, HD)
    return pl.pallas_call(
        kernel,
        out_shape=outs,
        grid_spec=pltpu.PrefetchScalarGridSpec(
            num_scalar_prefetch=1,
            grid=(len(heads),),
            in_specs=[
                whole((tokens, features)),
                pl.BlockSpec(weight, lambda i, o: (o[i, 0], 0, 0)),
                pl.BlockSpec(weight, lambda i, o: (o[i, 1], 0, 0)),
            ]
            + [whole(e.shape) for e in extra],
            out_specs=jax.tree.map(lambda s: whole(s.shape), outs),
        ),
        compiler_params=pltpu.CompilerParams(vmem_limit_bytes=32 * 2**20),
        cost_estimate=pl.CostEstimate(
            flops=2 * rows * features * 2 * HD * len(heads),
            bytes_accessed=2 * rows * features + 8 * features * HD * len(heads),
            transcendentals=0,
        ),
    )(picks, x, stack, stack, *extra)


def side_sum_kernel(local, two, one, three, keep, send):
    keep[...] = local[0] + (untriple(two[0]) + untriple(one[0])) + untriple(three[0])
    send[...] = triple(local[1] + (untriple(two[1]) + untriple(one[1])) + untriple(three[1]))


def join_kernel(local, two, one, three, side, got, out):
    first = local.shape[0]
    out[:first] = local[...] + (untriple(two[...]) + untriple(one[...])) + untriple(three[...])
    out[first:] = side[...] + untriple(got[...])


def call_whole(kernel, outs, *args):
    moved = sum(a.size * a.dtype.itemsize for a in args)
    return pl.pallas_call(
        kernel,
        out_shape=outs,
        compiler_params=pltpu.CompilerParams(vmem_limit_bytes=32 * 2**20),
        cost_estimate=pl.CostEstimate(flops=moved, bytes_accessed=2 * moved, transcendentals=0),
    )(*args)


FIRST = 576
TURN = (2, 1, 3, 0)


def after(value, *others):
    return lax.optimization_barrier((value, others))[0]


def project_far(x, stack, order):
    sent = jax.ShapeDtypeStruct((FIRST, 3 * HD), jnp.bfloat16)
    kernel = functools.partial(far_kernel, slice(0, FIRST))
    return project(kernel, order, x, stack, FIRST, [4 + k for k in TURN], (sent,) * 4)


def project_sides(x, stack, order):
    tokens = x.shape[0]
    rest = tokens - FIRST
    two_sent = jax.ShapeDtypeStruct((2, rest, 3 * HD), jnp.bfloat16)
    two_kept = jax.ShapeDtypeStruct((2, rest, 2 * HD), jnp.float32)
    heads = [d * 4 + k for k in TURN for d in range(2)]
    kernel = functools.partial(side_kernel, slice(FIRST, tokens))
    return project(kernel, order, x, stack, rest, heads, (two_sent,) * 3 + (two_kept,))


def send_sides(sides):
    return [tensor_perm(s, 0, 4 - k) for s, k in zip(sides[:3], TURN)]


def add_near(x, stack, order, got, back):
    shape = jax.ShapeDtypeStruct
    sent = shape((FIRST, 3 * HD), jnp.bfloat16)
    kept = shape((FIRST, 2 * HD), jnp.float32)
    parts = []
    got = [got[0], after(got[1], back[0]), after(got[2], back[1]), after(got[3], back[2])]
    for k, g in zip(TURN, got):
        kernel = functools.partial(near_kernel, k == 0, slice(0, FIRST))
        part = project(kernel, order, x, stack, FIRST, [k], kept if k == 0 else sent, (g,))
        parts.append(part)
    return parts


def send_near(parts):
    return [tensor_perm(p, 0, 4 - k) for p, k in zip(parts[:3], TURN)] + [parts[3]]


def add_sides(local, back):
    rest = local.shape[1]
    shape = jax.ShapeDtypeStruct
    outs = (shape((rest, 2 * HD), jnp.float32), shape((rest, 3 * HD), jnp.bfloat16))
    keep, send = call_whole(side_sum_kernel, outs, local, *back)
    return keep, tensor_perm(send, 1, 0)


def join(parts, keep, cross):
    *others, mine = parts
    out = jax.ShapeDtypeStruct((FIRST + keep.shape[0], 2 * HD), jnp.float32)
    return call_whole(join_kernel, out, mine, *others, keep, cross)


def weight_pieces(weight):
    across = dp_perm(weight, 1, 0)
    ahead = {k: dp_perm(weight, 0, k) for k in (2, 1, 3)}
    mine = [weight, ahead[1], ahead[2], ahead[3], across]
    mine += [dp_perm(across, 0, 1), dp_perm(ahead[2], 1, 0), dp_perm(across, 0, 3)]
    return jnp.stack(mine + [dp_perm(m, 0, 0, 1) for m in mine])


TAIL = 16


def coded(value):
    wide = jnp.full((TAIL, HD), value, jnp.float32)
    high = wide.astype(jnp.bfloat16).astype(jnp.float32)
    middle = (wide - high).astype(jnp.bfloat16).astype(jnp.float32)
    low = wide - high - middle
    lane = lax.broadcasted_iota(jnp.int32, (TAIL, HD), 1)
    return jnp.where(lane == 0, high, jnp.where(lane == 1, middle, jnp.where(lane == 2, low, 0.0))).astype(jnp.bfloat16)


def decoded(rows):
    return jnp.sum(rows[:1].astype(jnp.float32))


def grad_weight_kernel(picks, core, factors, xt_ref, d_ref, own_ref, other_ref):
    features, tokens = xt_ref.shape
    half = tokens // 2
    part = factors[0] * nn(xt_ref[:, :half], d_ref[0, :half])
    part = (part + factors[1] * nn(xt_ref[:, half:], d_ref[0, half:])).astype(jnp.bfloat16)
    keys, values = part[:, :HD], part[:, HD:]
    loss = coded(factors[2])
    own_ref[0, :features] = jnp.where(core[0] == 0, keys, values)
    own_ref[0, features:] = loss
    other_ref[0, :features] = jnp.where(core[0] == 0, values, keys)
    other_ref[0, features:] = loss


def grad_weight_terms(xt, dkv, picks, core, factors):
    features, tokens = xt.shape
    out = jax.ShapeDtypeStruct((8, features + TAIL, HD), jnp.bfloat16)
    spec = pl.BlockSpec((1, features + TAIL, HD), lambda i, *_: (i, 0, 0))
    return pl.pallas_call(
        grad_weight_kernel,
        out_shape=(out, out),
        grid_spec=pltpu.PrefetchScalarGridSpec(
            num_scalar_prefetch=3,
            grid=(8,),
            in_specs=[
                whole(xt.shape),
                pl.BlockSpec((1, tokens, 2 * HD), lambda i, p, *_: (p[i], 0, 0)),
            ],
            out_specs=(spec, spec),
        ),
        compiler_params=pltpu.CompilerParams(vmem_limit_bytes=32 * 2**20),
        cost_estimate=pl.CostEstimate(
            flops=2 * features * tokens * 16 * HD, bytes_accessed=10 * 2**20, transcendentals=0
        ),
    )(picks, core, factors, xt, dkv)


def pair_sum_kernel(own, other, *outs):
    features = own.shape[1] - TAIL
    for k, out in enumerate(outs):
        both = own[k, :features].astype(jnp.float32) + other[k, :features].astype(jnp.float32)
        out[:features] = both.astype(jnp.bfloat16)
        out[features:] = coded(decoded(own[k, features:]) + decoded(other[k, features:]))


def chip_sum_kernel(*refs):
    *parts, out, loss = refs
    features = out.shape[0]
    total = parts[0][:features].astype(jnp.float32)
    for p in parts[1:]:
        total = total + p[:features].astype(jnp.float32)
    out[...] = total
    v = [decoded(p[features:]) for p in parts]
    near, far = (v[0] + v[2]) + (v[1] + v[3]), (v[4] + v[6]) + (v[5] + v[7])
    loss[...] = jnp.full(loss.shape, near + far, jnp.float32)


def grad_input_kernel(order, factors, d_ref, w_ref, out_ref, turned):
    seq = pl.program_id(0)

    @pl.when(seq == 0)
    def _():
        for head in range(8):
            for kind in range(2):
                at = (2 * head + kind) * HD
                turned[:, at : at + HD] = w_ref[order[head, kind]]

    rows = jnp.concatenate([d_ref[head] for head in range(8)], axis=1)
    out_ref[...] = (factors[seq] * nt(rows, turned[...])).astype(jnp.bfloat16)


def grad_input_of(dkv, stack, order, factors):
    tokens, features = dkv.shape[1], stack.shape[1]
    half = tokens // 2
    return pl.pallas_call(
        grad_input_kernel,
        out_shape=jax.ShapeDtypeStruct((tokens, features), jnp.bfloat16),
        grid_spec=pltpu.PrefetchScalarGridSpec(
            num_scalar_prefetch=2,
            grid=(2,),
            in_specs=[pl.BlockSpec((8, half, 2 * HD), lambda s, *_: (0, s, 0)), whole(stack.shape)],
            out_specs=pl.BlockSpec((half, features), lambda s, *_: (s, 0)),
            scratch_shapes=[pltpu.VMEM((features, 16 * HD), jnp.bfloat16)],
        ),
        compiler_params=pltpu.CompilerParams(vmem_limit_bytes=40 * 2**20),
        cost_estimate=pl.CostEstimate(
            flops=2 * features * tokens * 16 * HD, bytes_accessed=12 * 2**20, transcendentals=0
        ),
    )(order, factors, dkv, stack)


def spread_heads(dkv):
    across = tensor_perm(dkv, 1, 0)
    ahead = {k: tensor_perm(dkv, 0, k) for k in (2, 1, 3)}
    mine = [dkv, ahead[1], ahead[2], ahead[3], across]
    mine += [tensor_perm(across, 0, 1), tensor_perm(ahead[2], 1, 0), tensor_perm(across, 0, 3)]
    return jnp.stack(mine), (across, ahead[1])


def reduce_terms(own, other):
    _, rows, columns = own.shape
    shape = jax.ShapeDtypeStruct
    totals = call_whole(
        pair_sum_kernel, (shape((rows, columns), own.dtype),) * 8, own, dp_perm(other, 0, 0, 1)
    )
    got = list(totals)
    for k, first in ((1, None), (3, None), (2, None), (4, None), (5, None), (6, 1), (7, 3)):
        part = totals[k] if first is None else after(totals[k], got[first])
        got[k] = dp_perm(part, k // 4, (4 - k % 4) % 4)
    return call_whole(
        chip_sum_kernel,
        (shape((rows - TAIL, columns), jnp.float32), shape((1, HD), jnp.float32)),
        *got,
    )


def on_device(
    policy_input,
    frozen_input,
    policy_query,
    frozen_query,
    readout,
    policy_weight,
    frozen_weight,
    resp_start,
    valid_len,
):
    place, head = lax.axis_index("dp"), lax.axis_index("tensor")
    x_hi, z, core = place // 8, place // 2 % 4, place % 2
    x_lo, y = head // 4, head % 4
    ends = jnp.concatenate([resp_start, valid_len], axis=0)
    near = jnp.arange(8, dtype=jnp.int32)
    heads = (x_lo ^ (near // 4)) * 4 + (y + near) % 4
    places = ((heads // 4) ^ x_hi) * 4 + (heads - z) % 4
    order = jnp.stack([places + 8 * core, places + 8 * (1 - core)], axis=1).astype(jnp.int32)
    frozen_order = jnp.stack([2 * heads, 2 * heads + 1], axis=1).astype(jnp.int32)
    targets = (x_hi ^ (near // 4)) * 4 + (z + near) % 4
    picks = (((targets // 4) ^ x_lo) * 4 + (targets - y) % 4).astype(jnp.int32)

    policy_stack = weight_pieces(policy_weight)
    frozen_stack = lax.all_gather(frozen_weight, "dp")
    xp, xf = policy_input, frozen_input
    far = project_far(xp, policy_stack, order)
    got = [tensor_perm(f, 1, 0) for f in far]
    *sides, local = project_sides(xp, policy_stack, order)
    back = send_sides(sides)
    parts = send_near(add_near(xp, policy_stack, order, got, back))
    frozen_stack = after(frozen_stack, parts[0])
    xt = after(policy_input, far).T
    keep, cross = add_sides(local, back)

    far_f = project_far(xf, frozen_stack, frozen_order)
    got_f = [tensor_perm(f, 1, 0) for f in far_f]
    *sides_f, local_f = project_sides(xf, frozen_stack, frozen_order)
    policy_kv = join(parts, keep, cross)
    back_f = send_sides(sides_f)
    first, first_sum = attention(True, 0, policy_kv, policy_query, readout, ends)
    policy_kv = after(policy_kv, got_f[0])
    second, second_sum = attention(True, 1, policy_kv, policy_query, readout, ends)
    dkv = jnp.concatenate([first, second])
    dkv = after(dkv, back_f[0])
    dkv_all, early = spread_heads(dkv)
    parts_f = send_near(add_near(xf, frozen_stack, frozen_order, got_f, back_f))
    keep_f, cross_f = add_sides(local_f, back_f)
    frozen_kv = join(parts_f, keep_f, cross_f)
    frozen_kv = after(frozen_kv, *early)
    sums = [attention(False, s, frozen_kv, frozen_query, readout, ends) for s in range(2)]
    gap = jnp.stack([jnp.sum(first_sum - sums[0]), jnp.sum(second_sum - sums[1])])
    gap = sum_tensor(jnp.broadcast_to(gap[:, None], (2, HD)))[:, 0]
    margin = BETA * (gap[0] - gap[1])
    sigma = jax.nn.sigmoid(-margin)
    factors = jnp.stack([-BETA * sigma, BETA * sigma, jax.nn.softplus(-margin)])
    own, other = grad_weight_terms(xt, dkv_all, picks, core.astype(jnp.int32).reshape(1), factors)
    grad_weight, loss = reduce_terms(own, other)
    grad_input = grad_input_of(dkv_all, policy_stack, order, factors)
    return (loss[0, 0], grad_weight, grad_input)


def solution(mesh):
    in_specs = (
        P("dp", "tensor"),
        P("dp", "tensor"),
        P("dp", "tensor"),
        P("dp", "tensor"),
        P("dp", "tensor"),
        P("tensor", "dp"),
        P("tensor", "dp"),
        P("dp", None),
        P("dp", None),
    )
    out_specs = (P(), P("tensor", "dp"), P("dp", "tensor"))
    return jax.shard_map(
        on_device, mesh=mesh, in_specs=in_specs, out_specs=out_specs, check_vma=False
    )
```

```python
import functools
import jax
import jax.numpy as jnp
from jax import lax
from jax.experimental import pallas as pl
from jax.experimental.pallas import tpu as pltpu
from jax.sharding import PartitionSpec as P

HD = 128
LEN = 512
HALF = LEN // 2
GROUPS = 8
LOG2E = 1.4426950408889634
NEGATIVE = -1e30
BETA = 0.1


def split_pair(wide):
    high = wide.astype(jnp.bfloat16)
    low = (wide - high.astype(jnp.float32)).astype(jnp.bfloat16)
    return jnp.concatenate([high, low], axis=1)


def nt(a, b):
    return lax.dot_general(a, b, (((1,), (1,)), ((), ())), preferred_element_type=jnp.float32)


def nn(a, b):
    return jnp.dot(a, b, preferred_element_type=jnp.float32)


def softmax_over_rows(scores, unit):
    highest = jnp.max(scores, axis=0, keepdims=True)
    expons = jnp.exp2((scores - highest) * unit)
    return expons * (1.0 / jnp.sum(expons, axis=0, keepdims=True))


def masked_scores(keys, query, block, valid):
    scores = nt(keys, jnp.concatenate([query, query], axis=1))
    rows = lax.broadcasted_iota(jnp.int32, (HALF, HALF), 0)
    cols = lax.broadcasted_iota(jnp.int32, (HALF, HALF), 1)
    if block == 0:
        return jnp.where(rows <= cols, scores, NEGATIVE)
    tail = jnp.where((rows <= cols) & (rows < valid - HALF), scores[HALF:], NEGATIVE)
    return jnp.concatenate([scores[:HALF], tail], axis=0)


def answered(block, begin, valid, read):
    places = lax.broadcasted_iota(jnp.int32, (HALF, 1), 0) + block * HALF
    return jnp.where((places >= begin) & (places < valid), read, jnp.zeros_like(read))


def policy_kernel(per, seq, ends, kv_ref, q_ref, r_ref, dkv_ref, lp_ref, keys, values, dk, dv):
    head = pl.program_id(0)
    begin, valid = ends[0, seq], ends[1, seq]
    factor = HD ** (-0.5)

    @pl.when(head == 0)
    def _():
        keys[...] = split_pair(kv_ref[:, :HD])
        values[...] = split_pair(kv_ref[:, HD:])
        dk[...] = jnp.zeros_like(dk)
        dv[...] = jnp.zeros_like(dv)
        lp_ref[...] = jnp.zeros_like(lp_ref)

    lp = jnp.zeros((1, HALF), jnp.float32)
    for h in range(per):
        for block in range(2):
            span = (block + 1) * HALF
            rows = slice(block * HALF, span)
            query = q_ref[rows, h * HD : (h + 1) * HD]
            read = answered(block, begin, valid, r_ref[rows, h * HD : (h + 1) * HD])
            weights = softmax_over_rows(
                masked_scores(keys[:span], query, block, valid), factor * LOG2E
            )
            rounded = weights.astype(jnp.bfloat16)
            dweights = nt(values[:span], jnp.concatenate([read, read], axis=1))
            inner = jnp.sum(rounded.astype(jnp.float32) * dweights, axis=0, keepdims=True)
            lp = lp + inner
            dscores = (weights * (dweights - inner)).astype(jnp.bfloat16)
            dv[:span] += nn(rounded, read)
            dk[:span] += nn(dscores, query)
    lp_ref[:1, :] += lp

    @pl.when(head == pl.num_programs(0) - 1)
    def _():
        dkv_ref[:, :HD] = (dk[...] * factor).astype(jnp.bfloat16)
        dkv_ref[:, HD:] = dv[...].astype(jnp.bfloat16)


def frozen_kernel(per, seq, ends, kv_ref, q_ref, r_ref, lp_ref, keys, values):
    head = pl.program_id(0)
    begin, valid = ends[0, seq], ends[1, seq]
    factor = HD ** (-0.5)

    @pl.when(head == 0)
    def _():
        keys[...] = split_pair(kv_ref[:, :HD])
        values[...] = split_pair(kv_ref[:, HD:])
        lp_ref[...] = jnp.zeros_like(lp_ref)

    lp = jnp.zeros((1, HALF), jnp.float32)
    for h in range(per):
        for block in range(2):
            span = (block + 1) * HALF
            rows = slice(block * HALF, span)
            query = q_ref[rows, h * HD : (h + 1) * HD]
            read = answered(block, begin, valid, r_ref[rows, h * HD : (h + 1) * HD])
            weights = softmax_over_rows(
                masked_scores(keys[:span], query, block, valid), factor * LOG2E
            )
            rounded = weights.astype(jnp.bfloat16)
            dweights = nt(values[:span], jnp.concatenate([read, read], axis=1))
            lp = lp + jnp.sum(rounded.astype(jnp.float32) * dweights, axis=0, keepdims=True)
    lp_ref[:1, :] += lp


def attention(policy, seq, kv, query, readout, ends, per=4):
    steps = GROUPS // per
    rows = lambda h, *_: (seq, 0)
    block = lambda h, *_: (seq, h)
    kernel = policy_kernel if policy else frozen_kernel
    lp_shape = jax.ShapeDtypeStruct((8, HALF), jnp.float32)
    lp_spec = pl.BlockSpec((8, HALF), lambda h, *_: (0, 0))
    scratch = [pltpu.VMEM((LEN, 2 * HD), jnp.bfloat16)] * 2
    flops = GROUPS * LEN * LEN * HD * 2 * (6 if policy else 4)
    if policy:
        out_shape = (jax.ShapeDtypeStruct((LEN, 2 * HD), jnp.bfloat16), lp_shape)
        out_specs = (pl.BlockSpec((LEN, 2 * HD), lambda h, *_: (0, 0)), lp_spec)
        scratch = scratch + [pltpu.VMEM((LEN, HD), jnp.float32)] * 2
    else:
        out_shape, out_specs = lp_shape, lp_spec
    out = pl.pallas_call(
        functools.partial(kernel, per, seq),
        out_shape=out_shape,
        grid_spec=pltpu.PrefetchScalarGridSpec(
            num_scalar_prefetch=1,
            grid=(steps,),
            in_specs=[
                pl.BlockSpec((LEN, 2 * HD), rows),
                pl.BlockSpec((LEN, per * HD), block),
                pl.BlockSpec((LEN, per * HD), block),
            ],
            out_specs=out_specs,
            scratch_shapes=scratch,
        ),
        compiler_params=pltpu.CompilerParams(vmem_limit_bytes=32 * 2**20),
        cost_estimate=pl.CostEstimate(
            flops=flops, bytes_accessed=5 * 2**19, transcendentals=GROUPS * LEN * LEN
        ),
        name="policy_attention" if policy else "frozen_attention",
    )(ends, kv, query, readout)
    return out


def tensor_perm(value, dx, dy):
    return lax.ppermute(
        value,
        "tensor",
        [(x * 4 + y, (x ^ dx) * 4 + (y - dy) % 4) for x in range(2) for y in range(4)],
    )


def dp_perm(value, dx, dz, dc=0):
    return lax.ppermute(
        value,
        "dp",
        [
            (x * 8 + z * 2 + c, (x ^ dx) * 8 + (z - dz) % 4 * 2 + (c ^ dc))
            for x in range(2)
            for z in range(4)
            for c in range(2)
        ],
    )


def sum_tensor(value):
    value = value + tensor_perm(value, 1, 0)
    ahead = [tensor_perm(value, 0, k) for k in (1, 2, 3)]
    return (value + ahead[1]) + (ahead[0] + ahead[2])


def triple(wide):
    keys = wide[:, :HD]
    high = keys.astype(jnp.bfloat16)
    low = (keys - high.astype(jnp.float32)).astype(jnp.bfloat16)
    return jnp.concatenate([high, low, wide[:, HD:].astype(jnp.bfloat16)], axis=1)


def untriple(sent):
    wide = sent.astype(jnp.float32)
    return jnp.concatenate([wide[:, :HD] + wide[:, HD : 2 * HD], wide[:, 2 * HD :]], axis=1)


def far_kernel(span, order, x_ref, k_ref, v_ref, *outs):
    step = pl.program_id(0)
    part = triple(nn(x_ref[span], jnp.concatenate([k_ref[0], v_ref[0]], axis=1)))
    for k, out in enumerate(outs):

        @pl.when(step == k)
        def _(out=out):
            out[...] = part


def side_kernel(span, order, x_ref, k_ref, v_ref, two, one, three, local):
    step = pl.program_id(0)
    part = nn(x_ref[span], jnp.concatenate([k_ref[0], v_ref[0]], axis=1))
    for k, out in enumerate((two, one, three)):

        @pl.when(step // 2 == k)
        def _(out=out):
            out[step % 2] = triple(part)

    @pl.when(step // 2 == 3)
    def _():
        local[step % 2] = part


def near_kernel(final, span, order, x_ref, k_ref, v_ref, got, out):
    part = nn(x_ref[span], jnp.concatenate([k_ref[0], v_ref[0]], axis=1)) + untriple(got[...])
    out[...] = part if final else triple(part)


def whole(shape):
    return pl.BlockSpec(shape, lambda *_: (0,) * len(shape))


def project(kernel, order, x, stack, rows, heads, outs, extra=()):
    tokens, features = x.shape
    picks = jnp.stack([order[h] for h in heads])
    weight = (1, features, HD)
    return pl.pallas_call(
        kernel,
        out_shape=outs,
        grid_spec=pltpu.PrefetchScalarGridSpec(
            num_scalar_prefetch=1,
            grid=(len(heads),),
            in_specs=[
                whole((tokens, features)),
                pl.BlockSpec(weight, lambda i, o: (o[i, 0], 0, 0)),
                pl.BlockSpec(weight, lambda i, o: (o[i, 1], 0, 0)),
            ]
            + [whole(e.shape) for e in extra],
            out_specs=jax.tree.map(lambda s: whole(s.shape), outs),
        ),
        compiler_params=pltpu.CompilerParams(vmem_limit_bytes=32 * 2**20),
        cost_estimate=pl.CostEstimate(
            flops=2 * rows * features * 2 * HD * len(heads),
            bytes_accessed=2 * rows * features + 8 * features * HD * len(heads),
            transcendentals=0,
        ),
    )(picks, x, stack, stack, *extra)


def side_sum_kernel(local, two, one, three, keep, send):
    keep[...] = local[0] + (untriple(two[0]) + untriple(one[0])) + untriple(three[0])
    send[...] = triple(local[1] + (untriple(two[1]) + untriple(one[1])) + untriple(three[1]))


def join_kernel(local, two, one, three, side, got, out):
    first = local.shape[0]
    out[:first] = local[...] + (untriple(two[...]) + untriple(one[...])) + untriple(three[...])
    out[first:] = side[...] + untriple(got[...])


def call_whole(kernel, outs, *args):
    moved = sum(a.size * a.dtype.itemsize for a in args)
    return pl.pallas_call(
        kernel,
        out_shape=outs,
        compiler_params=pltpu.CompilerParams(vmem_limit_bytes=32 * 2**20),
        cost_estimate=pl.CostEstimate(flops=moved, bytes_accessed=2 * moved, transcendentals=0),
    )(*args)


FIRST = 576
TURN = (2, 1, 3, 0)


def after(value, *others):
    return lax.optimization_barrier((value, others))[0]


def project_far(x, stack, order):
    sent = jax.ShapeDtypeStruct((FIRST, 3 * HD), jnp.bfloat16)
    kernel = functools.partial(far_kernel, slice(0, FIRST))
    return project(kernel, order, x, stack, FIRST, [4 + k for k in TURN], (sent,) * 4)


def project_sides(x, stack, order):
    tokens = x.shape[0]
    rest = tokens - FIRST
    two_sent = jax.ShapeDtypeStruct((2, rest, 3 * HD), jnp.bfloat16)
    two_kept = jax.ShapeDtypeStruct((2, rest, 2 * HD), jnp.float32)
    heads = [d * 4 + k for k in TURN for d in range(2)]
    kernel = functools.partial(side_kernel, slice(FIRST, tokens))
    return project(kernel, order, x, stack, rest, heads, (two_sent,) * 3 + (two_kept,))


def send_sides(sides):
    return [tensor_perm(s, 0, 4 - k) for s, k in zip(sides[:3], TURN)]


def add_near(x, stack, order, got, back):
    shape = jax.ShapeDtypeStruct
    sent = shape((FIRST, 3 * HD), jnp.bfloat16)
    kept = shape((FIRST, 2 * HD), jnp.float32)
    parts = []
    got = [got[0], after(got[1], back[0]), after(got[2], back[1]), after(got[3], back[2])]
    for k, g in zip(TURN, got):
        kernel = functools.partial(near_kernel, k == 0, slice(0, FIRST))
        part = project(kernel, order, x, stack, FIRST, [k], kept if k == 0 else sent, (g,))
        parts.append(part)
    return parts


def send_near(parts):
    return [tensor_perm(p, 0, 4 - k) for p, k in zip(parts[:3], TURN)] + [parts[3]]


def add_sides(local, back):
    rest = local.shape[1]
    shape = jax.ShapeDtypeStruct
    outs = (shape((rest, 2 * HD), jnp.float32), shape((rest, 3 * HD), jnp.bfloat16))
    keep, send = call_whole(side_sum_kernel, outs, local, *back)
    return keep, tensor_perm(send, 1, 0)


def join(parts, keep, cross):
    *others, mine = parts
    out = jax.ShapeDtypeStruct((FIRST + keep.shape[0], 2 * HD), jnp.float32)
    return call_whole(join_kernel, out, mine, *others, keep, cross)


def weight_pieces(weight):
    across = dp_perm(weight, 1, 0)
    ahead = {k: dp_perm(weight, 0, k) for k in (2, 1, 3)}
    mine = [weight, ahead[1], ahead[2], ahead[3], across]
    mine += [dp_perm(across, 0, 1), dp_perm(ahead[2], 1, 0), dp_perm(across, 0, 3)]
    return jnp.stack(mine + [dp_perm(m, 0, 0, 1) for m in mine])


TAIL = 16


def coded(value):
    wide = jnp.full((TAIL, HD), value, jnp.float32)
    high = wide.astype(jnp.bfloat16).astype(jnp.float32)
    middle = (wide - high).astype(jnp.bfloat16).astype(jnp.float32)
    low = wide - high - middle
    lane = lax.broadcasted_iota(jnp.int32, (TAIL, HD), 1)
    return jnp.where(lane == 0, high, jnp.where(lane == 1, middle, jnp.where(lane == 2, low, 0.0))).astype(jnp.bfloat16)


def decoded(rows):
    return jnp.sum(rows[:1].astype(jnp.float32))


def grad_weight_kernel(picks, core, factors, xt_ref, d_ref, own_ref, other_ref):
    features, tokens = xt_ref.shape
    half = tokens // 2
    part = factors[0] * nn(xt_ref[:, :half], d_ref[0, :half])
    part = (part + factors[1] * nn(xt_ref[:, half:], d_ref[0, half:])).astype(jnp.bfloat16)
    keys, values = part[:, :HD], part[:, HD:]
    loss = coded(factors[2])
    own_ref[0, :features] = jnp.where(core[0] == 0, keys, values)
    own_ref[0, features:] = loss
    other_ref[0, :features] = jnp.where(core[0] == 0, values, keys)
    other_ref[0, features:] = loss


def grad_weight_terms(xt, dkv, picks, core, factors):
    features, tokens = xt.shape
    count = picks.shape[0]
    out = jax.ShapeDtypeStruct((count, features + TAIL, HD), jnp.bfloat16)
    spec = pl.BlockSpec((1, features + TAIL, HD), lambda i, *_: (i, 0, 0))
    return pl.pallas_call(
        grad_weight_kernel,
        out_shape=(out, out),
        grid_spec=pltpu.PrefetchScalarGridSpec(
            num_scalar_prefetch=3,
            grid=(count,),
            in_specs=[
                whole(xt.shape),
                pl.BlockSpec((1, tokens, 2 * HD), lambda i, p, *_: (p[i], 0, 0)),
            ],
            out_specs=(spec, spec),
        ),
        compiler_params=pltpu.CompilerParams(vmem_limit_bytes=32 * 2**20),
        cost_estimate=pl.CostEstimate(
            flops=2 * features * tokens * 2 * count * HD, bytes_accessed=10 * 2**20, transcendentals=0
        ),
    )(picks, core, factors, xt, dkv)


def pair_sum_kernel(own, other, *outs):
    features = own.shape[1] - TAIL
    for k, out in enumerate(outs):
        both = own[k, :features].astype(jnp.float32) + other[k, :features].astype(jnp.float32)
        out[:features] = both.astype(jnp.bfloat16)
        out[features:] = coded(decoded(own[k, features:]) + decoded(other[k, features:]))


def chip_sum_kernel(*refs):
    *parts, out, loss = refs
    features = out.shape[0]
    total = parts[0][:features].astype(jnp.float32)
    for p in parts[1:]:
        total = total + p[:features].astype(jnp.float32)
    out[...] = total
    v = [decoded(p[features:]) for p in parts]
    near, far = (v[0] + v[2]) + (v[1] + v[3]), (v[4] + v[6]) + (v[5] + v[7])
    loss[...] = jnp.full(loss.shape, near + far, jnp.float32)


def grad_input_kernel(order, factors, d_ref, w_ref, out_ref, turned):
    seq = pl.program_id(0)

    @pl.when(seq == 0)
    def _():
        for head in range(8):
            for kind in range(2):
                at = (2 * head + kind) * HD
                turned[:, at : at + HD] = w_ref[order[head, kind]]

    rows = jnp.concatenate([d_ref[head] for head in range(8)], axis=1)
    out_ref[...] = (factors[seq] * nt(rows, turned[...])).astype(jnp.bfloat16)


def grad_input_of(dkv, stack, order, factors):
    tokens, features = dkv.shape[1], stack.shape[1]
    half = tokens // 2
    return pl.pallas_call(
        grad_input_kernel,
        out_shape=jax.ShapeDtypeStruct((tokens, features), jnp.bfloat16),
        grid_spec=pltpu.PrefetchScalarGridSpec(
            num_scalar_prefetch=2,
            grid=(2,),
            in_specs=[pl.BlockSpec((8, half, 2 * HD), lambda s, *_: (0, s, 0)), whole(stack.shape)],
            out_specs=pl.BlockSpec((half, features), lambda s, *_: (s, 0)),
            scratch_shapes=[pltpu.VMEM((features, 16 * HD), jnp.bfloat16)],
        ),
        compiler_params=pltpu.CompilerParams(vmem_limit_bytes=40 * 2**20),
        cost_estimate=pl.CostEstimate(
            flops=2 * features * tokens * 16 * HD, bytes_accessed=12 * 2**20, transcendentals=0
        ),
    )(order, factors, dkv, stack)


def spread_heads(dkv):
    across = tensor_perm(dkv, 1, 0)
    ahead = {k: tensor_perm(dkv, 0, k) for k in (2, 1, 3)}
    mine = [dkv, ahead[1], ahead[2], ahead[3], across]
    mine += [tensor_perm(across, 0, 1), tensor_perm(ahead[2], 1, 0), tensor_perm(across, 0, 3)]
    return jnp.stack(mine), (across, ahead[1])


def pair_terms(own, other):
    count, rows, columns = own.shape
    out = jax.ShapeDtypeStruct((rows, columns), own.dtype)
    return call_whole(pair_sum_kernel, (out,) * count, own, dp_perm(other, 0, 0, 1))


def reduce_terms(totals):
    rows, columns = totals[0].shape
    shape = jax.ShapeDtypeStruct
    got = list(totals)
    for k, first in ((4, None), (5, None), (7, None), (6, None), (1, None), (3, 4), (2, 5)):
        part = totals[k] if first is None else after(totals[k], got[first])
        got[k] = dp_perm(part, k // 4, (4 - k % 4) % 4)
    return call_whole(
        chip_sum_kernel,
        (shape((rows - TAIL, columns), jnp.float32), shape((1, HD), jnp.float32)),
        *got,
    )


def on_device(
    policy_input,
    frozen_input,
    policy_query,
    frozen_query,
    readout,
    policy_weight,
    frozen_weight,
    resp_start,
    valid_len,
):
    place, head = lax.axis_index("dp"), lax.axis_index("tensor")
    x_hi, z, core = place // 8, place // 2 % 4, place % 2
    x_lo, y = head // 4, head % 4
    ends = jnp.concatenate([resp_start, valid_len], axis=0)
    near = jnp.arange(8, dtype=jnp.int32)
    heads = (x_lo ^ (near // 4)) * 4 + (y + near) % 4
    places = ((heads // 4) ^ x_hi) * 4 + (heads - z) % 4
    order = jnp.stack([places + 8 * core, places + 8 * (1 - core)], axis=1).astype(jnp.int32)
    frozen_order = jnp.stack([2 * heads, 2 * heads + 1], axis=1).astype(jnp.int32)
    targets = (x_hi ^ (near // 4)) * 4 + (z + near) % 4
    picks = (((targets // 4) ^ x_lo) * 4 + (targets - y) % 4).astype(jnp.int32)

    policy_stack = weight_pieces(policy_weight)
    frozen_stack = lax.all_gather(frozen_weight, "dp")
    xp, xf = policy_input, frozen_input
    far = project_far(xp, policy_stack, order)
    got = [tensor_perm(f, 1, 0) for f in far]
    *sides, local = project_sides(xp, policy_stack, order)
    back = send_sides(sides)
    parts = send_near(add_near(xp, policy_stack, order, got, back))
    frozen_stack = after(frozen_stack, parts[0])
    xt = after(policy_input, far).T
    keep, cross = add_sides(local, back)

    far_f = project_far(xf, frozen_stack, frozen_order)
    got_f = [tensor_perm(f, 1, 0) for f in far_f]
    *sides_f, local_f = project_sides(xf, frozen_stack, frozen_order)
    policy_kv = join(parts, keep, cross)
    back_f = send_sides(sides_f)
    first, first_sum = attention(True, 0, policy_kv, policy_query, readout, ends)
    policy_kv = after(policy_kv, got_f[0])
    second, second_sum = attention(True, 1, policy_kv, policy_query, readout, ends)
    dkv = jnp.concatenate([first, second])
    dkv = after(dkv, back_f[0])
    dkv_all, early = spread_heads(dkv)
    parts_f = send_near(add_near(xf, frozen_stack, frozen_order, got_f, back_f))
    keep_f, cross_f = add_sides(local_f, back_f)
    frozen_kv = join(parts_f, keep_f, cross_f)
    frozen_kv = after(frozen_kv, *early)
    sums = [attention(False, s, frozen_kv, frozen_query, readout, ends) for s in range(2)]
    gap = jnp.stack([jnp.sum(first_sum - sums[0]), jnp.sum(second_sum - sums[1])])
    gap = sum_tensor(jnp.broadcast_to(gap[:, None], (2, HD)))[:, 0]
    margin = BETA * (gap[0] - gap[1])
    sigma = jax.nn.sigmoid(-margin)
    factors = jnp.stack([-BETA * sigma, BETA * sigma, jax.nn.softplus(-margin)])
    kind = core.astype(jnp.int32).reshape(1)
    across = pair_terms(*grad_weight_terms(xt, dkv_all, picks[4:], kind, factors))
    beside = pair_terms(*grad_weight_terms(xt, dkv_all, picks[:4], kind, factors))
    grad_weight, loss = reduce_terms([*beside, *across])
    grad_input = grad_input_of(dkv_all, policy_stack, order, factors)
    return (loss[0, 0], grad_weight, grad_input)


def solution(mesh):
    in_specs = (
        P("dp", "tensor"),
        P("dp", "tensor"),
        P("dp", "tensor"),
        P("dp", "tensor"),
        P("dp", "tensor"),
        P("tensor", "dp"),
        P("tensor", "dp"),
        P("dp", None),
        P("dp", None),
    )
    out_specs = (P(), P("tensor", "dp"), P("dp", "tensor"))
    return jax.shard_map(
        on_device, mesh=mesh, in_specs=in_specs, out_specs=out_specs, check_vma=False
    )
```
